32 devices in a mesh: src: 2 (over x), site: 16 (over z, y, core).
Axes of the slice: x: 2, y: 2, z: 4, core: 2. Of those that a mesh axis runs over, the one named last changes fastest.
Arguments:
- forward: bfloat16 [288, 65536], P(None, ('src', 'site')), parts along dimension 1, may hold values from -6 to 6
- seqprop: bfloat16 [512, 4608], P(('src', 'site')), parts along dimension 0, may hold values from -6 to 6
- sparse: int32 [4096], P(('src', 'site')), parts along dimension 0, may hold values from 0 to 2047, as said below
- owners: int32 [4096, 1], P(('src', 'site')), parts along dimension 0, may hold values from 0 to 15; in each aligned block of 128 rows (0 to 127, 128 to 255, ...) at most 16 rows name the same one
- contraction: int32 [1024, 6, 3], replicated, may hold values from 0 to 143
- momenta: int32 [64, 3], replicated, may hold values from -2 to 2
Outputs:
- corr: float32 [2048, 512], P(('src', 'site')), parts along dimension 0
The draws below stay inside these ranges and needn't reach their ends.
There are 2 independent parts, one for each index of `src`. The reference program is written for one: setup_inputs(seed, part) draws one part's arguments, and reference() takes and returns one part's arrays. A program takes and returns all parts, laid end to end along the dimension named above; an argument that names none is the same for every part. Nothing has to cross between parts.
Inputs may be any that keep to these rules, and one draw needn't show every extreme that they name: `sparse`: each device's 128 entries are distinct local site numbers. `owners`: among the 128 blocks of one device at most 16 name one owner.
All inputs are finite; a program needn't handle non-finite values.
Results may differ from the reference program's by a relative error of at most 0.0035.
Values may be sent and summed in bfloat16 or wider, within the bound.
A program may use at most 64 MiB of HBM per device.

```python
import math
import jax
import jax.numpy as jnp
import numpy as np
from jax import lax

LS = 64
MOMS = 64
K = 1024
TIMES = 4
SITES_DEV = 2048
BLK = 1
NBLK_DEV = 128
SEL_DEV = 128
CAP = 16
N_SITE = 16


def draw_sparse(key, part):
    key = jax.random.fold_in(key, 11)
    keys = jax.random.split(key, N_SITE)
    orders = jax.vmap(lambda single: jax.random.permutation(single, SITES_DEV))(keys)
    return orders[:, :SEL_DEV].reshape(-1).astype(jnp.int32)


def with_ends(values, rng, smallest, top_value):
    dims = values.shape
    spot = [jax.random.randint(jax.random.fold_in(rng, axis), (), 0, dims[axis]) for axis in range(len(dims))]
    values = values.at[tuple(spot)].set(smallest)
    longest = dims.index(max(dims))
    spot[longest] = (spot[longest] + 1) % dims[longest]
    return values.at[tuple(spot)].set(top_value)


def levels(rng, shape, pieces, low, high):
    factor_of = 1.0
    for dim, parts in pieces:
        draws = jax.random.uniform(jax.random.fold_in(jax.random.fold_in(rng, 6), dim), (parts,), jnp.float32, low / len(pieces), high / len(pieces))
        factor_of = factor_of * jnp.repeat(jnp.exp(draws), shape[dim] // parts).reshape((-1,) + (1,) * (len(shape) - 1 - dim))
    return factor_of


def shared_out(stream_key, own, number, rows, amount, top, reach, skew):
    sequence = jax.random.permutation(stream_key, amount)
    heavy_load, common = portions_of(amount, rows * top, reach, skew, True), portions_of(amount, rows * top, reach, skew, False)
    places = jnp.arange(amount)

    def named(tallies, turn):
        used = int((tallies > 0).sum())
        fixed = max(1, used // 4)
        passed = fixed + (places - fixed + turn * (used - fixed)) % max(1, amount - fixed)
        return jnp.zeros((amount,), jnp.int32).at[sequence[jnp.where(places < fixed, places, passed)]].set(jnp.asarray(tallies, jnp.int32))

    tallies = jnp.where(number % 4 == 0, named(heavy_load, number // 4), named(common, number - number // 4 - 1))
    mixed = jax.random.permutation(jax.random.fold_in(own, 3), amount)
    source_of, taker = mixed[0:amount // 2 * 2:2], mixed[1:amount // 2 * 2:2]
    slack = jnp.minimum(tallies[source_of] - 1, reach - tallies[taker]) // 2
    slack = jnp.where((source_of == sequence[0]) | (taker == sequence[0]) | (tallies[taker] == 0), 0, jnp.maximum(slack, 0))
    passed = jax.random.randint(jax.random.fold_in(own, 4), (amount // 2,), 0, 1 << 20) % (slack + 1)
    tallies = tallies.at[source_of].add(-passed).at[taker].add(passed)
    members = jnp.searchsorted(jnp.cumsum(tallies), jnp.arange(rows * top), side="right").astype(jnp.int32)
    table = members.reshape(top, rows).T
    table = table[jax.random.permutation(jax.random.fold_in(own, 1), rows)]
    turn = jax.random.randint(jax.random.fold_in(own, 2), (rows, 1), 0, top)
    return jnp.take_along_axis(table, (jnp.arange(top)[None, :] + turn) % top, axis=1)


def portions_of(count, total, most, slope, full):
    portions = [(1 << 20) // math.isqrt(standing ** slope) + 1 for standing in range(1, count + 1)]
    largest = most if full else min(most, max(-(-total // count), total * portions[0] // sum(portions)))
    least = 1 if total - largest >= count - 1 else 0
    counts, surplus = [largest] + [least] * (count - 1), total - largest - least * (count - 1)
    while surplus > 0:
        candidates = [i for i in range(1, count) if counts[i] < largest] or [i for i in range(1, count) if counts[i] < most]
        whole, remaining = sum([portions[i] for i in candidates]), surplus
        for i in candidates:
            more = min(most - counts[i], max(1, remaining * portions[i] // whole), surplus)
            counts[i] = counts[i] + more
            surplus = surplus - more
    return np.array(counts)


def noise(key, shape, scale, bound, cuts=(), kind=jnp.bfloat16):
    values = jax.random.normal(key, shape, jnp.float32) * scale
    if len(cuts) > 0:
        values = levels(key, shape, cuts, -0.22, 0.18) * values
    return jnp.clip(values, min=-bound, max=bound).astype(kind)


def setup_inputs(seed: int = 0, part: int = 0) -> dict:
    seeds = jax.random.split(jax.random.key(seed), 7)
    part_splits = jax.random.split(jax.random.fold_in(seeds[6], part), 7)
    forward = noise(part_splits[0], (288, N_SITE * SITES_DEV), 1.0, 6.0, ((1, 16),))
    seqprop = noise(part_splits[1], (N_SITE * N_SITE, 288 * CAP * BLK), 1.0, 6.0, ((0, 16),))
    sparse = draw_sparse(jax.random.fold_in(jax.random.fold_in(seeds[6], part), 71), part)
    owners_keys = jax.random.split(jax.random.fold_in(part_splits[3], 1), (N_SITE * NBLK_DEV) // NBLK_DEV)
    owners_turns = jax.random.permutation(jax.random.fold_in(part_splits[3], 3), (N_SITE * NBLK_DEV) // NBLK_DEV)
    owners = jax.vmap(lambda own, number: shared_out(jax.random.fold_in(part_splits[3], 2), own, number, NBLK_DEV, N_SITE, 1, CAP, 2))(owners_keys, owners_turns).reshape((N_SITE * NBLK_DEV, 1))
    contraction = with_ends(jax.random.randint(seeds[4], (K, 6, 3), 0, 144), jax.random.fold_in(seeds[4], 1), 0, 143).astype(jnp.int32)
    momenta = with_ends(jax.random.randint(seeds[5], (MOMS, 3), -2, 3), jax.random.fold_in(seeds[5], 1), -2, 2).astype(jnp.int32)
    return dict(forward=forward, seqprop=seqprop, sparse=sparse, owners=owners, contraction=contraction, momenta=momenta)


def slot_ranks(owner_row, count):
    onehot = (owner_row[:, None] == jnp.arange(count, dtype=jnp.int32)[None, :]).astype(jnp.int32)
    before = jnp.cumsum(onehot, axis=0) - onehot
    return lax.optimization_barrier(jnp.sum(before * onehot, axis=1)).astype(jnp.int32)

def phase_table(glob, momenta, sites_dev, nsite):
    device = glob // sites_dev
    per_time = nsite // TIMES
    tslice = device // per_time
    spatial = device % per_time * sites_dev + glob % sites_dev
    coord_x = spatial % LS
    coord_y = spatial // LS % LS
    coord_z = spatial // (LS * LS) % LS
    dotted = coord_x[:, None] * momenta[None, :, 0] + coord_y[:, None] * momenta[None, :, 1] + coord_z[:, None] * momenta[None, :, 2]
    angle = (dotted % LS).astype(jnp.float32) * (2.0 * math.pi / LS)
    inside = (tslice[:, None] == jnp.arange(TIMES, dtype=jnp.int32)[None, :]).astype(jnp.float32)
    real_part = (inside[:, :, None] * jnp.cos(angle)[:, None, :]).reshape(glob.shape[0], TIMES * MOMS)
    imag_part = (-inside[:, :, None] * jnp.sin(angle)[:, None, :]).reshape(glob.shape[0], TIMES * MOMS)
    return (real_part.astype(jnp.bfloat16), imag_part.astype(jnp.bfloat16))

def contract(left, right, table):
    half = left.shape[0] // 2
    fre, fim, sre, sim = (left[:half], left[half:], right[:half], right[half:])
    acc_re = jnp.zeros((table.shape[0], left.shape[1]), jnp.float32)
    acc_im = jnp.zeros((table.shape[0], left.shape[1]), jnp.float32)
    for term in range(6):
        sign = 1.0 if term < 3 else -1.0
        ia, ib, ic = (table[:, term, 0], table[:, term, 1], table[:, term, 2])
        ar, ai = (fre[ia].astype(jnp.float32), fim[ia].astype(jnp.float32))
        br, bi = (fre[ib].astype(jnp.float32), fim[ib].astype(jnp.float32))
        cr, ci = (sre[ic].astype(jnp.float32), sim[ic].astype(jnp.float32))
        pr = ar * br - ai * bi
        pi = ar * bi + ai * br
        acc_re = acc_re + sign * (pr * cr - pi * ci)
        acc_im = acc_im + sign * (pr * ci + pi * cr)
    return (acc_re.astype(jnp.bfloat16), acc_im.astype(jnp.bfloat16))

def project(bre, bim, wre, wim):
    first = jnp.dot(bre, wre, preferred_element_type=jnp.float32) - jnp.dot(bim, wim, preferred_element_type=jnp.float32)
    second = jnp.dot(bre, wim, preferred_element_type=jnp.float32) + jnp.dot(bim, wre, preferred_element_type=jnp.float32)
    return jnp.concatenate([first, second], axis=1)

def reference(forward, seqprop, sparse, owners, contraction, momenta):
    comps = forward.shape[0]

    def one(total, device):
        local = lax.dynamic_slice_in_dim(sparse, device * SEL_DEV, SEL_DEV)
        block_fwd = lax.dynamic_slice_in_dim(forward, device * SITES_DEV, SITES_DEV, 1)
        fsel = jnp.take(block_fwd, local, axis=1)
        owner_row = lax.dynamic_slice_in_dim(owners[:, 0], device * NBLK_DEV, NBLK_DEV)
        slot = slot_ranks(owner_row, N_SITE)
        rows = seqprop[owner_row * N_SITE + device].reshape(NBLK_DEV, comps, CAP, BLK)
        picked = rows[jnp.arange(NBLK_DEV, dtype=jnp.int32), :, slot, :]
        right = jnp.transpose(picked, (1, 0, 2)).reshape(comps, SEL_DEV)
        glob = device * SITES_DEV + local
        wre, wim = phase_table(glob, momenta, SITES_DEV, N_SITE)
        bre, bim = contract(fsel, right, contraction)
        return (total + project(bre, bim, wre, wim), None)
    start = jnp.zeros((K, 2 * TIMES * MOMS), jnp.float32)
    total, _ = lax.scan(one, start, jnp.arange(N_SITE, dtype=jnp.int32))
    return total / jnp.sqrt(jnp.float32(SEL_DEV * N_SITE / TIMES))
```

```python
import functools
import math

import jax
import jax.numpy as jnp
from jax import lax
from jax.experimental import pallas as pl
from jax.experimental.pallas import tpu as pltpu
from jax.sharding import PartitionSpec as P

LS = 64
TIMES = 4
TERMS = 6
LANES = 128
DEPTH = 256
ROWS = 128
F32 = jnp.float32
BF16 = jnp.bfloat16
I32 = jnp.int32


def iota(shape, dim):
    return lax.broadcasted_iota(I32, shape, dim)


def onehot(mask):
    return jnp.where(mask, 1.0, 0.0).astype(BF16)


def column(row):
    n = row.shape[1]
    return jnp.broadcast_to(row.astype(F32), (n, n)).T.astype(I32)


def kernel(
    nsite,
    fwd_ref,
    seq_ref,
    sparse_ref,
    owner_ref,
    table_ref,
    mom_ref,
    out_ref,
    msg32,
    msgs,
    got,
    tabs,
    tabt,
    tf,
    ts,
    phase,
    ohf,
    ohs,
    gat,
    prod,
    parts,
    acc,
    send1,
    recv1,
    send2,
    recv2,
):
    me = lax.axis_index("site")
    comps, sites_dev = fwd_ref.shape
    half = comps // 2
    sel = sparse_ref.shape[1]
    slots = seq_ref.shape[1] // comps
    kall = table_ref.shape[2]
    kdev = kall // nsite
    moms = mom_ref.shape[1]
    per_time = nsite // TIMES
    pitch = msgs.shape[1]

    barrier = pltpu.get_barrier_semaphore()

    def greet(step, _):
        dst = lax.rem(me + step, nsite)
        pl.semaphore_signal(
            barrier, inc=1, device_id={"site": dst}, device_id_type=pl.DeviceIdType.MESH
        )
        return 0

    lax.fori_loop(1, nsite, greet, 0)

    flat = seq_ref.shape[1]
    for c in range(pitch):
        low = c * LANES
        if low >= flat:
            piece = jnp.zeros((nsite, LANES), F32)
        else:
            width = min(LANES, flat - low)
            piece = seq_ref[:, low : low + width].astype(F32)
            if width < LANES:
                piece = jnp.concatenate([piece, jnp.zeros((nsite, LANES - width), F32)], axis=1)
        msg32[pl.ds(c, nsite, stride=pitch), :] = piece
    msgs[...] = msg32[...].reshape(nsite, pitch, LANES).astype(BF16)

    pl.semaphore_wait(barrier, nsite - 1)

    def seq_copy(slot, peer):
        return pltpu.make_async_remote_copy(
            src_ref=msgs.at[peer],
            dst_ref=got.at[slot],
            send_sem=send1.at[peer],
            recv_sem=recv1.at[slot],
            device_id={"site": peer},
            device_id_type=pl.DeviceIdType.MESH,
        )

    def send_seq(step, _):
        dst = lax.rem(me + step, nsite)
        seq_copy(me, dst).start()
        return 0

    lax.fori_loop(1, nsite, send_seq, 0)
    got[me] = msgs[me]

    sparse = sparse_ref[...]
    pick = onehot(iota((sites_dev, sel), 0) == sparse)
    fsel = jnp.dot(fwd_ref[...], pick, preferred_element_type=F32).astype(BF16)
    tf[...] = jnp.zeros_like(tf)
    tf[0:half, 0:sel] = fsel[:half]
    tf[0:half, sel:] = fsel[half:]

    tabs[...] = jnp.zeros_like(tabs)
    for m in range(TERMS):
        tabs[3 * m : 3 * m + 3, :] = table_ref[m].astype(F32)
    for c in range(kall // LANES):
        tabt[c * LANES : (c + 1) * LANES, :] = tabs[:, c * LANES : (c + 1) * LANES].T.astype(I32)

    def forward_part(ci, _):
        base = pl.multiple_of(ci * ROWS, ROWS)
        idx = tabt[pl.ds(base, ROWS), :]
        lane = iota((ROWS, DEPTH), 1)
        for m in range(TERMS):
            for f in range(2):
                low = (2 * m + f) * ROWS
                ohf[low : low + ROWS, :] = onehot(idx[:, 3 * m + f : 3 * m + f + 1] == lane)
            low = m * ROWS
            ohs[ci, low : low + ROWS, :] = onehot(idx[:, 3 * m + 2 : 3 * m + 3] == lane)
        gat[...] = jnp.dot(ohf[...], tf[...], preferred_element_type=F32)
        for m in range(TERMS):
            la, lb, low = 2 * m * ROWS, (2 * m + 1) * ROWS, m * ROWS
            ar, ai = gat[la : la + ROWS, :sel], gat[la : la + ROWS, sel:]
            br, bi = gat[lb : lb + ROWS, :sel], gat[lb : lb + ROWS, sel:]
            prod[ci, low : low + ROWS, :sel] = ar * br - ai * bi
            prod[ci, low : low + ROWS, sel:] = ar * bi + ai * br
        return 0

    lax.fori_loop(0, kall // ROWS, forward_part, 0)

    spatial = lax.rem(me, per_time) * sites_dev + column(sparse)
    xs, ys, zs = spatial & (LS - 1), (spatial >> 6) & (LS - 1), (spatial >> 12) & (LS - 1)
    mom = mom_ref[...]
    mom = jnp.concatenate([mom, mom], axis=1)
    dotted = xs * mom[0:1] + ys * mom[1:2] + zs * mom[2:3]
    second = iota((sel, 2 * moms), 1) >= moms
    quarter = LS // 4
    for part in range(2):
        shift = jnp.where(second, quarter, 0) - quarter * part
        angle = ((dotted + shift) & (LS - 1)).astype(F32) * (2.0 * math.pi / LS)
        phase[part * sel : (part + 1) * sel, :] = jnp.cos(angle).astype(BF16)

    owner = owner_ref[...]
    earlier = (column(owner) == owner) & (iota((sel, sel), 0) < iota((sel, sel), 1))
    rank = jnp.sum(jnp.where(earlier, 1.0, 0.0), axis=0, keepdims=True).astype(I32)
    key = owner * slots + rank

    def wait_seq(step, _):
        src = lax.rem(me + nsite - step, nsite)
        seq_copy(src, src).wait_recv()
        return 0

    lax.fori_loop(1, nsite, wait_seq, 0)

    per_row = LANES // slots

    def select(o, total):
        rows = got[o].astype(F32)
        pieces = []
        group = iota((8, LANES), 1) // slots
        for g in range(comps // 8):
            row = g * 8 // per_row
            want = g * 8 % per_row + iota((8, LANES), 0)
            line = jnp.broadcast_to(rows[row : row + 1, :], (8, LANES))
            pieces.append(jnp.where(group == want, line, 0.0))
        spread = jnp.concatenate(pieces, axis=0).astype(BF16)
        match = onehot(o * slots + iota((LANES, sel), 0) % slots == key)
        return total + jnp.dot(spread, match, preferred_element_type=F32)

    ssel = lax.fori_loop(0, nsite, select, jnp.zeros((comps, sel), F32)).astype(BF16)
    ts[...] = jnp.zeros_like(ts)
    ts[0:half, 0:sel] = ssel[:half]
    ts[0:half, sel:] = ssel[half:]

    def part_copy(slot, peer):
        return pltpu.make_async_remote_copy(
            src_ref=parts.at[peer],
            dst_ref=acc.at[slot],
            send_sem=send2.at[peer],
            recv_sem=recv2.at[slot],
            device_id={"site": peer},
            device_id_type=pl.DeviceIdType.MESH,
        )

    kpad = parts.shape[1]
    nchunks = kall // ROWS
    mine = me * kdev // ROWS

    def finish(step, _):
        ci = lax.rem(mine + 1 + step, nchunks)
        gs = jnp.dot(ohs[ci], ts[...], preferred_element_type=F32)
        re = jnp.zeros((ROWS, sel), F32)
        im = jnp.zeros((ROWS, sel), F32)
        for m in range(TERMS):
            low = m * ROWS
            cr, cim = gs[low : low + ROWS, :sel], gs[low : low + ROWS, sel:]
            pr, pim = prod[ci, low : low + ROWS, :sel], prod[ci, low : low + ROWS, sel:]
            tr, tim = pr * cr - pim * cim, pr * cim + pim * cr
            if m < 3:
                re, im = re + tr, im + tim
            else:
                re, im = re - tr, im - tim
        block = jnp.concatenate([re, im], axis=1).astype(BF16)
        sums = jnp.dot(block, phase[...], preferred_element_type=F32)
        for h in range(ROWS // kdev):
            piece = sums[h * kdev : (h + 1) * kdev]
            if kpad > kdev:
                piece = jnp.concatenate([piece, jnp.zeros((kpad - kdev, LANES), F32)], axis=0)
            dst = ci * (ROWS // kdev) + h
            parts[dst] = piece.astype(BF16)

            @pl.when(dst != me)
            def _():
                part_copy(me, dst).start()

        return 0

    lax.fori_loop(0, nchunks, finish, 0)
    acc[me] = parts[me]

    def wait_part(step, _):
        src = lax.rem(me + nsite - step, nsite)
        part_copy(src, src).wait_recv()
        return 0

    lax.fori_loop(1, nsite, wait_part, 0)

    scale = 1.0 / math.sqrt(sel * nsite / TIMES)
    firsts, seconds = [], []
    for t in range(TIMES):
        total = jnp.zeros((kpad, LANES), F32)
        for g in range(per_time):
            total = total + acc[t * per_time + g].astype(F32)
        total = total[:kdev] * scale
        firsts.append(total[:, :moms])
        seconds.append(total[:, moms:])
    out_ref[...] = jnp.concatenate(firsts + seconds, axis=1)

    def drain(step, _):
        dst = lax.rem(me + step, nsite)
        seq_copy(me, dst).wait_send()
        part_copy(me, dst).wait_send()
        return 0

    lax.fori_loop(1, nsite, drain, 0)


def shards(forward, seqprop, sparse, owners, contraction, momenta):
    nsite = lax.axis_size("site")
    comps = forward.shape[0]
    kept = sparse.shape[0]
    kall = contraction.shape[0]
    moms = momenta.shape[0]
    flat = seqprop.shape[1]
    pitch = -(-flat // (16 * LANES)) * 16
    kdev = kall // nsite
    kpad = max(16, kdev)
    nchunks = kall // ROWS
    vmem = pl.BlockSpec(memory_space=pltpu.VMEM)
    return pl.pallas_call(
        functools.partial(kernel, nsite),
        out_shape=jax.ShapeDtypeStruct((kdev, 2 * TIMES * moms), F32),
        in_specs=[vmem] * 6,
        out_specs=vmem,
        scratch_shapes=[
            pltpu.VMEM((nsite * pitch, LANES), F32),
            pltpu.VMEM((nsite, pitch, LANES), BF16),
            pltpu.VMEM((nsite, pitch, LANES), BF16),
            pltpu.VMEM((LANES, kall), F32),
            pltpu.VMEM((kall, LANES), I32),
            pltpu.VMEM((DEPTH, 2 * kept), BF16),
            pltpu.VMEM((DEPTH, 2 * kept), BF16),
            pltpu.VMEM((2 * kept, 2 * moms), BF16),
            pltpu.VMEM((2 * TERMS * ROWS, DEPTH), BF16),
            pltpu.VMEM((nchunks, TERMS * ROWS, DEPTH), BF16),
            pltpu.VMEM((2 * TERMS * ROWS, 2 * kept), F32),
            pltpu.VMEM((nchunks, TERMS * ROWS, 2 * kept), F32),
            pltpu.VMEM((nsite, kpad, LANES), BF16),
            pltpu.VMEM((nsite, kpad, LANES), BF16),
            pltpu.SemaphoreType.DMA((nsite,)),
            pltpu.SemaphoreType.DMA((nsite,)),
            pltpu.SemaphoreType.DMA((nsite,)),
            pltpu.SemaphoreType.DMA((nsite,)),
        ],
        compiler_params=pltpu.CompilerParams(
            collective_id=0, has_side_effects=True, vmem_limit_bytes=48 * 1024 * 1024
        ),
    )(
        forward,
        seqprop,
        sparse.reshape(1, kept),
        owners.T,
        jnp.transpose(contraction, (1, 2, 0)),
        momenta.T,
    )


def solution(mesh):
    return jax.shard_map(
        shards,
        mesh=mesh,
        in_specs=(
            P(None, ("src", "site")),
            P(("src", "site"), None),
            P(("src", "site")),
            P(("src", "site"), None),
            P(),
            P(),
        ),
        out_specs=P(("src", "site"), None),
        check_vma=False,
    )
```

```python
import functools
import math

import jax
import jax.numpy as jnp
from jax import lax
from jax.experimental import pallas as pl
from jax.experimental.pallas import tpu as pltpu
from jax.sharding import PartitionSpec as P

LS = 64
TIMES = 4
TERMS = 6
LANES = 128
DEPTH = 256
ROWS = 128
LAG = 3
EARLY = 2
F32 = jnp.float32
BF16 = jnp.bfloat16
I32 = jnp.int32


def iota(shape, dim):
    return lax.broadcasted_iota(I32, shape, dim)


def onehot(mask):
    return jnp.where(mask, 1.0, 0.0).astype(BF16)


def column(row):
    n = row.shape[1]
    return jnp.broadcast_to(row.astype(F32), (n, n)).T.astype(I32)


def kernel(
    nsite,
    fwd_hbm,
    seq_hbm,
    sparse_hbm,
    owner_hbm,
    table_hbm,
    mom_hbm,
    out_ref,
    fwd_ref,
    seq_ref,
    sparse_ref,
    owner_ref,
    table_ref,
    mom_ref,
    load_sem,
    msg32,
    msgs,
    got,
    tabs,
    tabt,
    tf,
    ts,
    phase,
    ohf,
    ohs,
    gat,
    prod,
    halves,
    others,
    parts,
    acc,
    send1,
    recv1,
    send2,
    recv2,
    send3,
    recv3,
):
    me = lax.axis_index("site")
    comps, sites_dev = fwd_ref.shape
    half = comps // 2
    sel = sparse_ref.shape[1]
    slots = seq_ref.shape[1] // comps
    kall = table_ref.shape[2]
    kdev = kall // nsite
    moms = mom_ref.shape[1]
    per_time = nsite // TIMES
    pitch = msgs.shape[1]

    loads = [
        pltpu.make_async_copy(source, target, load_sem.at[n])
        for n, (source, target) in enumerate(
            [
                (seq_hbm, seq_ref),
                (sparse_hbm, sparse_ref),
                (fwd_hbm, fwd_ref),
                (table_hbm, table_ref),
                (owner_hbm, owner_ref),
                (mom_hbm, mom_ref),
            ]
        )
    ]
    for load in loads:
        load.start()

    barrier = pltpu.get_barrier_semaphore()

    def greet(step, _):
        dst = lax.rem(me + step, nsite)
        pl.semaphore_signal(
            barrier, inc=1, device_id={"site": dst}, device_id_type=pl.DeviceIdType.MESH
        )
        return 0

    lax.fori_loop(1, nsite, greet, 0)

    loads[0].wait()
    flat = seq_ref.shape[1]
    for c in range(pitch):
        low = c * LANES
        if low >= flat:
            piece = jnp.zeros((nsite, LANES), F32)
        else:
            width = min(LANES, flat - low)
            piece = seq_ref[:, low : low + width].astype(F32)
            if width < LANES:
                piece = jnp.concatenate([piece, jnp.zeros((nsite, LANES - width), F32)], axis=1)
        msg32[pl.ds(c, nsite, stride=pitch), :] = piece
    msgs[...] = msg32[...].reshape(nsite, pitch, LANES).astype(BF16)

    for load in loads[1:]:
        load.wait()

    sparse = sparse_ref[...]
    pick = onehot(iota((sites_dev, sel), 0) == sparse)
    fsel = jnp.dot(fwd_ref[...], pick, preferred_element_type=F32).astype(BF16)
    tf[...] = jnp.zeros_like(tf)
    tf[0:half, 0:sel] = fsel[:half]
    tf[0:half, sel:] = fsel[half:]

    tabs[...] = jnp.zeros_like(tabs)
    for m in range(TERMS):
        tabs[3 * m : 3 * m + 3, :] = table_ref[m].astype(F32)
    for c in range(kall // LANES):
        tabt[c * LANES : (c + 1) * LANES, :] = tabs[:, c * LANES : (c + 1) * LANES].T.astype(I32)

    def forward_part(ci, _):
        base = pl.multiple_of(ci * ROWS, ROWS)
        idx = tabt[pl.ds(base, ROWS), :]
        lane = iota((ROWS, DEPTH), 1)
        for m in range(TERMS):
            for f in range(2):
                low = (2 * m + f) * ROWS
                ohf[low : low + ROWS, :] = onehot(idx[:, 3 * m + f : 3 * m + f + 1] == lane)
            low = m * ROWS
            ohs[ci, low : low + ROWS, :] = onehot(idx[:, 3 * m + 2 : 3 * m + 3] == lane)
        gat[...] = jnp.dot(ohf[...], tf[...], preferred_element_type=F32)
        for m in range(TERMS):
            la, lb, low = 2 * m * ROWS, (2 * m + 1) * ROWS, m * ROWS
            ar, ai = gat[la : la + ROWS, :sel], gat[la : la + ROWS, sel:]
            br, bi = gat[lb : lb + ROWS, :sel], gat[lb : lb + ROWS, sel:]
            prod[ci, low : low + ROWS, :sel] = ar * br - ai * bi
            prod[ci, low : low + ROWS, sel:] = ar * bi + ai * br
        return 0

    lax.fori_loop(0, EARLY, forward_part, 0)
    pl.semaphore_wait(barrier, nsite - 1)

    def seq_copy(slot, peer):
        return pltpu.make_async_remote_copy(
            src_ref=msgs.at[peer],
            dst_ref=got.at[slot],
            send_sem=send1.at[peer],
            recv_sem=recv1.at[slot],
            device_id={"site": peer},
            device_id_type=pl.DeviceIdType.MESH,
        )

    def send_seq(step, _):
        dst = lax.rem(me + step, nsite)
        seq_copy(me, dst).start()
        return 0

    lax.fori_loop(1, nsite, send_seq, 0)
    got[me] = msgs[me]

    lax.fori_loop(EARLY, kall // ROWS, forward_part, 0)

    spatial = lax.rem(me, per_time) * sites_dev + column(sparse)
    xs, ys, zs = spatial & (LS - 1), (spatial >> 6) & (LS - 1), (spatial >> 12) & (LS - 1)
    mom = mom_ref[...]
    mom = jnp.concatenate([mom, mom], axis=1)
    dotted = xs * mom[0:1] + ys * mom[1:2] + zs * mom[2:3]
    second = iota((sel, 2 * moms), 1) >= moms
    quarter = LS // 4
    for part in range(2):
        shift = jnp.where(second, quarter, 0) - quarter * part
        angle = ((dotted + shift) & (LS - 1)).astype(F32) * (2.0 * math.pi / LS)
        phase[part * sel : (part + 1) * sel, :] = jnp.cos(angle).astype(BF16)

    owner = owner_ref[...]
    earlier = (column(owner) == owner) & (iota((sel, sel), 0) < iota((sel, sel), 1))
    rank = jnp.sum(jnp.where(earlier, 1.0, 0.0), axis=0, keepdims=True).astype(I32)
    key = owner * slots + rank

    per_row = LANES // slots

    def select(step, total):
        o = lax.rem(me + nsite - step, nsite)

        @pl.when(step > 0)
        def _():
            seq_copy(o, o).wait_recv()

        rows = got[o].astype(F32)
        pieces = []
        group = iota((8, LANES), 1) // slots
        for g in range(comps // 8):
            row = g * 8 // per_row
            want = g * 8 % per_row + iota((8, LANES), 0)
            line = jnp.broadcast_to(rows[row : row + 1, :], (8, LANES))
            pieces.append(jnp.where(group == want, line, 0.0))
        spread = jnp.concatenate(pieces, axis=0).astype(BF16)
        match = onehot(o * slots + iota((LANES, sel), 0) % slots == key)
        return total + jnp.dot(spread, match, preferred_element_type=F32)

    ssel = lax.fori_loop(0, nsite, select, jnp.zeros((comps, sel), F32)).astype(BF16)
    ts[...] = jnp.zeros_like(ts)
    ts[0:half, 0:sel] = ssel[:half]
    ts[0:half, sel:] = ssel[half:]

    core = lax.rem(me, 2)
    partner = me + 1 - 2 * core
    chip = me // 2
    nchips = nsite // 2

    def pair_copy(peer):
        return pltpu.make_async_remote_copy(
            src_ref=halves.at[peer],
            dst_ref=others.at[peer],
            send_sem=send3.at[peer],
            recv_sem=recv3.at[peer],
            device_id={"site": partner},
            device_id_type=pl.DeviceIdType.MESH,
        )

    def part_copy(slot, peer):
        return pltpu.make_async_remote_copy(
            src_ref=parts.at[peer],
            dst_ref=acc.at[slot],
            send_sem=send2.at[peer],
            recv_sem=recv2.at[slot],
            device_id={"site": 2 * peer + core},
            device_id_type=pl.DeviceIdType.MESH,
        )

    kpad = parts.shape[1]
    nchunks = kall // ROWS
    mine = me * kdev // ROWS
    per_chunk = ROWS // kdev // 2

    def chunk_at(step):
        return lax.rem(mine + 1 + step, nchunks)

    def forward_sums(step):
        ci = chunk_at(step)
        for h in range(per_chunk):
            target = ci * per_chunk + h
            pair_copy(target).wait_recv()
            parts[target] = (halves[nchips + target] + others[target]).astype(BF16)

            @pl.when(target != chip)
            def _():
                part_copy(chip, target).start()

    def finish(step, _):
        ci = chunk_at(step)
        gs = jnp.dot(ohs[ci], ts[...], preferred_element_type=F32)
        re = jnp.zeros((ROWS, sel), F32)
        im = jnp.zeros((ROWS, sel), F32)
        for m in range(TERMS):
            low = m * ROWS
            cr, cim = gs[low : low + ROWS, :sel], gs[low : low + ROWS, sel:]
            pr, pim = prod[ci, low : low + ROWS, :sel], prod[ci, low : low + ROWS, sel:]
            tr, tim = pr * cr - pim * cim, pr * cim + pim * cr
            if m < 3:
                re, im = re + tr, im + tim
            else:
                re, im = re - tr, im - tim
        block = jnp.concatenate([re, im], axis=1).astype(BF16)
        sums = jnp.dot(block, phase[...], preferred_element_type=F32)
        for h in range(per_chunk):
            target = ci * per_chunk + h
            low = 2 * h * kdev
            even, odd = sums[low : low + kdev], sums[low + kdev : low + 2 * kdev]
            if kpad > kdev:
                blank = jnp.zeros((kpad - kdev, LANES), F32)
                even = jnp.concatenate([even, blank], axis=0)
                odd = jnp.concatenate([odd, blank], axis=0)
            halves[target] = jnp.where(core == 0, odd, even)
            halves[nchips + target] = jnp.where(core == 0, even, odd)
            pair_copy(target).start()

        @pl.when(step >= LAG)
        def _():
            forward_sums(step - LAG)

        return 0

    lax.fori_loop(0, nchunks, finish, 0)
    for step in range(nchunks - LAG, nchunks):
        forward_sums(step)
    acc[chip] = parts[chip]

    def wait_part(step, _):
        src = lax.rem(chip + nchips - step, nchips)
        part_copy(src, src).wait_recv()
        return 0

    lax.fori_loop(1, nchips, wait_part, 0)

    scale = 1.0 / math.sqrt(sel * nsite / TIMES)
    firsts, seconds = [], []
    for t in range(TIMES):
        total = jnp.zeros((kpad, LANES), F32)
        for g in range(per_time // 2):
            total = total + acc[t * (per_time // 2) + g].astype(F32)
        total = total[:kdev] * scale
        firsts.append(total[:, :moms])
        seconds.append(total[:, moms:])
    out_ref[...] = jnp.concatenate(firsts + seconds, axis=1)

    def drain(step, _):
        dst = lax.rem(me + step, nsite)
        seq_copy(me, dst).wait_send()
        return 0

    lax.fori_loop(1, nsite, drain, 0)

    def drain_pairs(target, _):
        pair_copy(target).wait_send()

        @pl.when(target != chip)
        def _():
            part_copy(chip, target).wait_send()

        return 0

    lax.fori_loop(0, nchips, drain_pairs, 0)


def shards(forward, seqprop, sparse, owners, contraction, momenta):
    nsite = lax.axis_size("site")
    comps = forward.shape[0]
    kept = sparse.shape[0]
    kall = contraction.shape[0]
    moms = momenta.shape[0]
    flat = seqprop.shape[1]
    pitch = -(-flat // (16 * LANES)) * 16
    kdev = kall // nsite
    kpad = max(16, kdev)
    nchunks = kall // ROWS
    vmem = pl.BlockSpec(memory_space=pltpu.VMEM)
    return pl.pallas_call(
        functools.partial(kernel, nsite),
        out_shape=jax.ShapeDtypeStruct((kdev, 2 * TIMES * moms), F32),
        in_specs=[pl.BlockSpec(memory_space=pltpu.HBM)] * 6,
        out_specs=vmem,
        scratch_shapes=[
            pltpu.VMEM(forward.shape, BF16),
            pltpu.VMEM(seqprop.shape, BF16),
            pltpu.VMEM((1, kept), I32),
            pltpu.VMEM((1, kept), I32),
            pltpu.VMEM((TERMS, 3, kall), I32),
            pltpu.VMEM((3, moms), I32),
            pltpu.SemaphoreType.DMA((6,)),
            pltpu.VMEM((nsite * pitch, LANES), F32),
            pltpu.VMEM((nsite, pitch, LANES), BF16),
            pltpu.VMEM((nsite, pitch, LANES), BF16),
            pltpu.VMEM((LANES, kall), F32),
            pltpu.VMEM((kall, LANES), I32),
            pltpu.VMEM((DEPTH, 2 * kept), BF16),
            pltpu.VMEM((DEPTH, 2 * kept), BF16),
            pltpu.VMEM((2 * kept, 2 * moms), BF16),
            pltpu.VMEM((2 * TERMS * ROWS, DEPTH), BF16),
            pltpu.VMEM((nchunks, TERMS * ROWS, DEPTH), BF16),
            pltpu.VMEM((2 * TERMS * ROWS, 2 * kept), F32),
            pltpu.VMEM((nchunks, TERMS * ROWS, 2 * kept), F32),
            pltpu.VMEM((nsite, kpad, LANES), F32),
            pltpu.VMEM((nsite // 2, kpad, LANES), F32),
            pltpu.VMEM((nsite // 2, kpad, LANES), BF16),
            pltpu.VMEM((nsite // 2, kpad, LANES), BF16),
            pltpu.SemaphoreType.DMA((nsite,)),
            pltpu.SemaphoreType.DMA((nsite,)),
            pltpu.SemaphoreType.DMA((nsite // 2,)),
            pltpu.SemaphoreType.DMA((nsite // 2,)),
            pltpu.SemaphoreType.DMA((nsite // 2,)),
            pltpu.SemaphoreType.DMA((nsite // 2,)),
        ],
        compiler_params=pltpu.CompilerParams(
            collective_id=0, has_side_effects=True, vmem_limit_bytes=63 * 1024 * 1024
        ),
    )(
        forward,
        seqprop,
        sparse.reshape(1, kept),
        owners.T,
        jnp.transpose(contraction, (1, 2, 0)),
        momenta.T,
    )


def solution(mesh):
    return jax.shard_map(
        shards,
        mesh=mesh,
        in_specs=(
            P(None, ("src", "site")),
            P(("src", "site"), None),
            P(("src", "site")),
            P(("src", "site"), None),
            P(),
            P(),
        ),
        out_specs=P(("src", "site"), None),
        check_vma=False,
    )
```

```python
import functools
import math

import jax
import jax.numpy as jnp
from jax import lax
from jax.experimental import pallas as pl
from jax.experimental.pallas import tpu as pltpu
from jax.sharding import PartitionSpec as P

LS = 64
TIMES = 4
TERMS = 6
LANES = 128
DEPTH = 256
ROWS = 128
LAG = 3
EARLY = 2
F32 = jnp.float32
BF16 = jnp.bfloat16
I32 = jnp.int32


def iota(shape, dim):
    return lax.broadcasted_iota(I32, shape, dim)


def onehot(mask):
    return jnp.where(mask, 1.0, 0.0).astype(BF16)


def column(row):
    n = row.shape[1]
    return jnp.broadcast_to(row.astype(F32), (n, n)).T.astype(I32)


def kernel(
    nsite,
    fwd_hbm,
    seq_hbm,
    sparse_hbm,
    owner_hbm,
    table_hbm,
    mom_hbm,
    out_ref,
    fwd_ref,
    seq_ref,
    sparse_ref,
    owner_ref,
    table_ref,
    mom_ref,
    load_sem,
    msg32,
    msgs,
    got,
    tabs,
    tabt,
    tf,
    ts,
    phase,
    ohf,
    ohs,
    gat,
    prod,
    halves,
    others,
    parts,
    acc,
    send1,
    recv1,
    send2,
    recv2,
    send3,
    recv3,
):
    me = lax.axis_index("site")
    comps, sites_dev = fwd_ref.shape
    half = comps // 2
    sel = sparse_ref.shape[1]
    slots = seq_ref.shape[1] // comps
    kall = table_ref.shape[2]
    kdev = kall // nsite
    moms = mom_ref.shape[1]
    per_time = nsite // TIMES
    pitch = msgs.shape[1]

    loads = [
        pltpu.make_async_copy(source, target, load_sem.at[n])
        for n, (source, target) in enumerate(
            [
                (seq_hbm, seq_ref),
                (sparse_hbm, sparse_ref),
                (fwd_hbm, fwd_ref),
                (table_hbm, table_ref),
                (owner_hbm, owner_ref),
                (mom_hbm, mom_ref),
            ]
        )
    ]
    for load in loads:
        load.start()

    barrier = pltpu.get_barrier_semaphore()

    def greet(step, _):
        dst = lax.rem(me + step, nsite)
        pl.semaphore_signal(
            barrier, inc=1, device_id={"site": dst}, device_id_type=pl.DeviceIdType.MESH
        )
        return 0

    lax.fori_loop(1, nsite, greet, 0)

    loads[0].wait()
    flat = seq_ref.shape[1]
    for c in range(pitch):
        low = c * LANES
        if low >= flat:
            piece = jnp.zeros((nsite, LANES), F32)
        else:
            width = min(LANES, flat - low)
            piece = seq_ref[:, low : low + width].astype(F32)
            if width < LANES:
                piece = jnp.concatenate([piece, jnp.zeros((nsite, LANES - width), F32)], axis=1)
        msg32[pl.ds(c, nsite, stride=pitch), :] = piece
    msgs[...] = msg32[...].reshape(nsite, pitch, LANES).astype(BF16)

    for load in loads[1:]:
        load.wait()

    sparse = sparse_ref[...]
    pick = onehot(iota((sites_dev, sel), 0) == sparse)
    fsel = jnp.dot(fwd_ref[...], pick, preferred_element_type=F32).astype(BF16)
    tf[...] = jnp.zeros_like(tf)
    tf[0:half, 0:sel] = fsel[:half]
    tf[0:half, sel:] = fsel[half:]

    tabs[...] = jnp.zeros_like(tabs)
    for m in range(TERMS):
        tabs[3 * m : 3 * m + 3, :] = table_ref[m].astype(F32)
    for c in range(kall // LANES):
        tabt[c * LANES : (c + 1) * LANES, :] = tabs[:, c * LANES : (c + 1) * LANES].T.astype(I32)

    def forward_part(ci, _):
        base = pl.multiple_of(ci * ROWS, ROWS)
        idx = tabt[pl.ds(base, ROWS), :]
        lane = iota((ROWS, DEPTH), 1)
        for m in range(TERMS):
            for f in range(2):
                low = (2 * m + f) * ROWS
                ohf[low : low + ROWS, :] = onehot(idx[:, 3 * m + f : 3 * m + f + 1] == lane)
            low = m * ROWS
            ohs[ci, low : low + ROWS, :] = onehot(idx[:, 3 * m + 2 : 3 * m + 3] == lane)
        gat[...] = jnp.dot(ohf[...], tf[...], preferred_element_type=F32)
        for m in range(TERMS):
            la, lb, low = 2 * m * ROWS, (2 * m + 1) * ROWS, m * ROWS
            ar, ai = gat[la : la + ROWS, :sel], gat[la : la + ROWS, sel:]
            br, bi = gat[lb : lb + ROWS, :sel], gat[lb : lb + ROWS, sel:]
            prod[ci, low : low + ROWS, :sel] = ar * br - ai * bi
            prod[ci, low : low + ROWS, sel:] = ar * bi + ai * br
        return 0

    lax.fori_loop(0, EARLY, forward_part, 0)
    pl.semaphore_wait(barrier, nsite - 1)

    def seq_copy(slot, peer):
        return pltpu.make_async_remote_copy(
            src_ref=msgs.at[peer],
            dst_ref=got.at[slot],
            send_sem=send1.at[peer],
            recv_sem=recv1.at[slot],
            device_id={"site": peer},
            device_id_type=pl.DeviceIdType.MESH,
        )

    def send_seq(step, _):
        dst = lax.rem(me + step, nsite)
        seq_copy(me, dst).start()
        return 0

    lax.fori_loop(1, nsite, send_seq, 0)
    got[me] = msgs[me]

    lax.fori_loop(EARLY, kall // ROWS, forward_part, 0)

    spatial = lax.rem(me, per_time) * sites_dev + column(sparse)
    xs, ys, zs = spatial & (LS - 1), (spatial >> 6) & (LS - 1), (spatial >> 12) & (LS - 1)
    mom = mom_ref[...]
    mom = jnp.concatenate([mom, mom], axis=1)
    dotted = xs * mom[0:1] + ys * mom[1:2] + zs * mom[2:3]
    second = iota((sel, 2 * moms), 1) >= moms
    quarter = LS // 4
    for part in range(2):
        shift = jnp.where(second, quarter, 0) - quarter * part
        angle = ((dotted + shift) & (LS - 1)).astype(F32) * (2.0 * math.pi / LS)
        phase[part * sel : (part + 1) * sel, :] = jnp.cos(angle).astype(BF16)

    owner = owner_ref[...]
    earlier = (column(owner) == owner) & (iota((sel, sel), 0) < iota((sel, sel), 1))
    rank = jnp.sum(jnp.where(earlier, 1.0, 0.0), axis=0, keepdims=True).astype(I32)
    key = owner * slots + rank

    per_row = LANES // slots

    def select(step, total):
        o = lax.rem(me + nsite - step, nsite)

        @pl.when(step > 0)
        def _():
            seq_copy(o, o).wait_recv()

        rows = got[o].astype(F32)
        pieces = []
        group = iota((8, LANES), 1) // slots
        for g in range(comps // 8):
            row = g * 8 // per_row
            want = g * 8 % per_row + iota((8, LANES), 0)
            line = jnp.broadcast_to(rows[row : row + 1, :], (8, LANES))
            pieces.append(jnp.where(group == want, line, 0.0))
        spread = jnp.concatenate(pieces, axis=0).astype(BF16)
        match = onehot(o * slots + iota((LANES, sel), 0) % slots == key)
        return total + jnp.dot(spread, match, preferred_element_type=F32)

    ssel = lax.fori_loop(0, nsite, select, jnp.zeros((comps, sel), F32), unroll=4).astype(BF16)
    ts[...] = jnp.zeros_like(ts)
    ts[0:half, 0:sel] = ssel[:half]
    ts[0:half, sel:] = ssel[half:]

    core = lax.rem(me, 2)
    partner = me + 1 - 2 * core
    chip = me // 2
    nchips = nsite // 2

    def pair_copy(peer):
        return pltpu.make_async_remote_copy(
            src_ref=halves.at[peer],
            dst_ref=others.at[peer],
            send_sem=send3.at[peer],
            recv_sem=recv3.at[peer],
            device_id={"site": partner},
            device_id_type=pl.DeviceIdType.MESH,
        )

    def part_copy(slot, peer):
        return pltpu.make_async_remote_copy(
            src_ref=parts.at[peer],
            dst_ref=acc.at[slot],
            send_sem=send2.at[peer],
            recv_sem=recv2.at[slot],
            device_id={"site": 2 * peer + core},
            device_id_type=pl.DeviceIdType.MESH,
        )

    kpad = parts.shape[1]
    nchunks = kall // ROWS
    mine = me * kdev // ROWS
    per_chunk = ROWS // kdev // 2

    def chunk_at(step):
        return lax.rem(mine + 1 + step, nchunks)

    def forward_sums(step):
        ci = chunk_at(step)
        for h in range(per_chunk):
            target = ci * per_chunk + h
            pair_copy(target).wait_recv()
            parts[target] = (halves[nchips + target] + others[target]).astype(BF16)

            @pl.when(target != chip)
            def _():
                part_copy(chip, target).start()

    def finish(step, _):
        ci = chunk_at(step)
        gs = jnp.dot(ohs[ci], ts[...], preferred_element_type=F32)
        re = jnp.zeros((ROWS, sel), F32)
        im = jnp.zeros((ROWS, sel), F32)
        for m in range(TERMS):
            low = m * ROWS
            cr, cim = gs[low : low + ROWS, :sel], gs[low : low + ROWS, sel:]
            pr, pim = prod[ci, low : low + ROWS, :sel], prod[ci, low : low + ROWS, sel:]
            tr, tim = pr * cr - pim * cim, pr * cim + pim * cr
            if m < 3:
                re, im = re + tr, im + tim
            else:
                re, im = re - tr, im - tim
        block = jnp.concatenate([re, im], axis=1).astype(BF16)
        sums = jnp.dot(block, phase[...], preferred_element_type=F32)
        for h in range(per_chunk):
            target = ci * per_chunk + h
            low = 2 * h * kdev
            even, odd = sums[low : low + kdev], sums[low + kdev : low + 2 * kdev]
            if kpad > kdev:
                blank = jnp.zeros((kpad - kdev, LANES), F32)
                even = jnp.concatenate([even, blank], axis=0)
                odd = jnp.concatenate([odd, blank], axis=0)
            halves[target] = jnp.where(core == 0, odd, even)
            halves[nchips + target] = jnp.where(core == 0, even, odd)
            pair_copy(target).start()

        @pl.when(step >= LAG)
        def _():
            forward_sums(step - LAG)

        return 0

    lax.fori_loop(0, nchunks, finish, 0)
    for step in range(nchunks - LAG, nchunks):
        forward_sums(step)
    acc[chip] = parts[chip]

    def wait_part(step, _):
        src = lax.rem(chip + nchips - step, nchips)
        part_copy(src, src).wait_recv()
        return 0

    lax.fori_loop(1, nchips, wait_part, 0)

    scale = 1.0 / math.sqrt(sel * nsite / TIMES)
    firsts, seconds = [], []
    for t in range(TIMES):
        total = jnp.zeros((kpad, LANES), F32)
        for g in range(per_time // 2):
            total = total + acc[t * (per_time // 2) + g].astype(F32)
        total = total[:kdev] * scale
        firsts.append(total[:, :moms])
        seconds.append(total[:, moms:])
    out_ref[...] = jnp.concatenate(firsts + seconds, axis=1)

    def drain(step, _):
        dst = lax.rem(me + step, nsite)
        seq_copy(me, dst).wait_send()
        return 0

    lax.fori_loop(1, nsite, drain, 0)

    def drain_pairs(target, _):
        pair_copy(target).wait_send()

        @pl.when(target != chip)
        def _():
            part_copy(chip, target).wait_send()

        return 0

    lax.fori_loop(0, nchips, drain_pairs, 0)


def shards(forward, seqprop, sparse, owners, contraction, momenta):
    nsite = lax.axis_size("site")
    comps = forward.shape[0]
    kept = sparse.shape[0]
    kall = contraction.shape[0]
    moms = momenta.shape[0]
    flat = seqprop.shape[1]
    pitch = -(-flat // (16 * LANES)) * 16
    kdev = kall // nsite
    kpad = max(16, kdev)
    nchunks = kall // ROWS
    vmem = pl.BlockSpec(memory_space=pltpu.VMEM)
    return pl.pallas_call(
        functools.partial(kernel, nsite),
        out_shape=jax.ShapeDtypeStruct((kdev, 2 * TIMES * moms), F32),
        in_specs=[pl.BlockSpec(memory_space=pltpu.HBM)] * 6,
        out_specs=vmem,
        scratch_shapes=[
            pltpu.VMEM(forward.shape, BF16),
            pltpu.VMEM(seqprop.shape, BF16),
            pltpu.VMEM((1, kept), I32),
            pltpu.VMEM((1, kept), I32),
            pltpu.VMEM((TERMS, 3, kall), I32),
            pltpu.VMEM((3, moms), I32),
            pltpu.SemaphoreType.DMA((6,)),
            pltpu.VMEM((nsite * pitch, LANES), F32),
            pltpu.VMEM((nsite, pitch, LANES), BF16),
            pltpu.VMEM((nsite, pitch, LANES), BF16),
            pltpu.VMEM((LANES, kall), F32),
            pltpu.VMEM((kall, LANES), I32),
            pltpu.VMEM((DEPTH, 2 * kept), BF16),
            pltpu.VMEM((DEPTH, 2 * kept), BF16),
            pltpu.VMEM((2 * kept, 2 * moms), BF16),
            pltpu.VMEM((2 * TERMS * ROWS, DEPTH), BF16),
            pltpu.VMEM((nchunks, TERMS * ROWS, DEPTH), BF16),
            pltpu.VMEM((2 * TERMS * ROWS, 2 * kept), F32),
            pltpu.VMEM((nchunks, TERMS * ROWS, 2 * kept), F32),
            pltpu.VMEM((nsite, kpad, LANES), F32),
            pltpu.VMEM((nsite // 2, kpad, LANES), F32),
            pltpu.VMEM((nsite // 2, kpad, LANES), BF16),
            pltpu.VMEM((nsite // 2, kpad, LANES), BF16),
            pltpu.SemaphoreType.DMA((nsite,)),
            pltpu.SemaphoreType.DMA((nsite,)),
            pltpu.SemaphoreType.DMA((nsite // 2,)),
            pltpu.SemaphoreType.DMA((nsite // 2,)),
            pltpu.SemaphoreType.DMA((nsite // 2,)),
            pltpu.SemaphoreType.DMA((nsite // 2,)),
        ],
        compiler_params=pltpu.CompilerParams(
            collective_id=0, has_side_effects=True, vmem_limit_bytes=63 * 1024 * 1024
        ),
    )(
        forward,
        seqprop,
        sparse.reshape(1, kept),
        owners.T,
        jnp.transpose(contraction, (1, 2, 0)),
        momenta.T,
    )


def solution(mesh):
    return jax.shard_map(
        shards,
        mesh=mesh,
        in_specs=(
            P(None, ("src", "site")),
            P(("src", "site"), None),
            P(("src", "site")),
            P(("src", "site"), None),
            P(),
            P(),
        ),
        out_specs=P(("src", "site"), None),
        check_vma=False,
    )
```
